32 devices in a mesh: pipe: 4 (over z), dp: 4 (over x, core), fsdp: 2 (over y).
Axes of the slice: x: 2, y: 2, z: 4, core: 2. Of those that a mesh axis runs over, the one named last changes fastest.
Arguments:
- layer_inputs: bfloat16 [4, 2, 2048, 4096], P('pipe', None, ('dp', 'fsdp')), may hold values from -6 to 6
- key_grads: bfloat16 [4, 2, 2048, 512], P('pipe', None, ('dp', 'fsdp')), may hold values from -12 to 12
- token_counts: int32 [4, 16], P('pipe', ('dp', 'fsdp')), may hold values from 1 to 256, 2048 in all within a row
- master_weight: float32 [4, 4096, 512], P('pipe', 'fsdp'), may hold values from -0.09375 to 0.09375
- first_moment: float32 [4, 4096, 512], P('pipe', 'fsdp'), may hold values from -3 to 3
- second_moment: float32 [4, 4096, 512], P('pipe', 'fsdp'), may hold values from 0.05 to 2
Outputs:
- input_grads: bfloat16 [4, 2, 2048, 4096], P('pipe', None, ('dp', 'fsdp'))
- new_weight: float32 [4, 4096, 512], P('pipe', 'fsdp')
- new_first: float32 [4, 4096, 512], P('pipe', 'fsdp')
- new_second: float32 [4, 4096, 512], P('pipe', 'fsdp')
The draws below stay inside these ranges and needn't reach their ends.
Inputs may be any that keep to these rules, and one draw needn't show every extreme that they name: `token_counts`: in each section the counts sum to 2048, and some microbatch of each section is full.
All inputs are finite; a program needn't handle non-finite values. No bound on the sum of `token_counts` on one device may be relied on, other than what follows from the above.
Results may differ from the reference program's by a relative error of at most 0.00105.
The reference program's roundings to bfloat16 on the way count: a program that leaves them out, or rounds other values in their place, can miss the bound.
Values may be sent and summed in bfloat16 or wider, within the bound.
A program may use at most 128 MiB of HBM per device.

```python
import math
import jax
import jax.numpy as jnp
import numpy as np
from jax import lax

D = 4096
KV = 512
MB = 2
TOK = 256
REPL = 8
TOKENS = 2048
N_PIPE = 4
N_DP = 4
N_FSDP = 2


def block_scale(own_key, shape, pieces, low, largest):
    gain = 1.0
    for position, blocks in pieces:
        heights = jax.random.uniform(jax.random.fold_in(jax.random.fold_in(own_key, 6), position), (blocks,), jnp.float32, low / len(pieces), largest / len(pieces))
        gain = gain * jnp.repeat(jnp.exp(heights), shape[position] // blocks).reshape((-1,) + (1,) * (len(shape) - 1 - position))
    return gain


def length_profile(count, total, reach, slope):
    portions = [(1 << 20) // math.isqrt(standing ** slope) + 1 for standing in range(2, count + 1)]
    surplus, given = total - reach - (count - 1), [1] * (count - 1)
    while surplus > 0:
        movable = [i for i in range(count - 1) if given[i] < reach]
        mass, left = sum([portions[i] for i in movable]), surplus
        for i in movable:
            addition = min(reach - given[i], max(1, left * portions[i] // mass), surplus)
            given[i] = given[i] + addition
            surplus = surplus - addition
    return np.array([reach] + given)


def ragged_sizes(key, count, total, bound, skew):
    if count == 2:
        one = jax.random.randint(key, (), max(1, total - bound), min(bound, total - 1) + 1)
        return jnp.stack([one, total - one])
    lengths = jnp.asarray(length_profile(count, total, bound, skew), jnp.int32)
    pairs = (count - 1) // 2
    giver, taker = lengths[1:1 + 2 * pairs:2], lengths[2:2 + 2 * pairs:2]
    slack = jnp.minimum(giver - 1, bound - taker)
    shifted = jax.random.randint(jax.random.fold_in(key, 1), (pairs,), 0, 1 << 20) % (slack + 1)
    lengths = lengths.at[1:1 + 2 * pairs:2].set(giver - shifted).at[2:2 + 2 * pairs:2].set(taker + shifted)
    return lengths[jax.random.permutation(jax.random.fold_in(key, 2), count)]


def noise(key, dims, width, reach, split=(), kind=jnp.bfloat16):
    factor_of = block_scale(key, dims, split, -0.22, 0.18) if split else 1.0
    entries = jax.random.normal(key, dims, jnp.float32) * width * factor_of
    return jnp.minimum(jnp.maximum(entries, -reach), reach).astype(kind)


def setup_inputs(seed: int = 0) -> dict:
    seeds = jax.random.split(jax.random.key(seed), 7)
    layer_inputs = noise(seeds[0], (N_PIPE, MB, TOKENS, D), 1.0, 6.0, ((0, 4), (2, 8)))
    key_grads = noise(seeds[1], (N_PIPE, MB, TOKENS, KV), 2.0, 12.0, ((0, 4), (2, 8)))
    token_counts = jax.vmap(lambda own: ragged_sizes(own, REPL * MB, N_DP * N_FSDP * MB * TOK // 2, TOK, 2))(jax.random.split(seeds[2], N_PIPE)).reshape((N_PIPE, REPL * MB)).astype(jnp.int32)
    master_weight = noise(seeds[3], (N_PIPE, D, KV), D ** -0.5, 0.09375, ((0, 4), (1, 2)), jnp.float32)
    first_moment = noise(seeds[4], (N_PIPE, D, KV), 0.5, 3.0, ((0, 4), (1, 2)), jnp.float32)
    second_moment = jnp.clip(jnp.exp(math.log(2.0) - 3.6888794 * jax.random.uniform(seeds[5], (N_PIPE, D, KV), jnp.float32) ** block_scale(seeds[5], (N_PIPE, D, KV), ((0, 4), (1, 2)), -0.2, 0.2)), 0.05, 2.0)
    return dict(layer_inputs=layer_inputs, key_grads=key_grads, token_counts=token_counts, master_weight=master_weight, first_moment=first_moment, second_moment=second_moment)


beta_one = 0.9
beta_two = 0.95
learn_rate = 0.01
decay_rate = 0.1
adam_eps = 1e-08
loss_scale = 256.0
first_bias = 1.0 - 0.9 ** 10
second_bias = 1.0 - 0.95 ** 10

def adamw_update(weight_part, first_part, second_part, gradient):
    first_next = beta_one * first_part + (1.0 - beta_one) * gradient
    second_next = beta_two * second_part + (1.0 - beta_two) * gradient * gradient
    first_hat = first_next / first_bias
    second_hat = second_next / second_bias
    weight_next = weight_part - learn_rate * (first_hat / (jnp.sqrt(second_hat) + adam_eps) + decay_rate * weight_part)
    return (weight_next, first_next, second_next)

def reference(layer_inputs, key_grads, token_counts, master_weight, first_moment, second_moment):
    positions = jnp.arange(TOK, dtype=jnp.int32)
    incoming = jnp.zeros((MB, TOKENS, D), jnp.bfloat16)
    grad_list = [None] * N_PIPE
    weight_list = [None] * N_PIPE
    first_list = [None] * N_PIPE
    second_list = [None] * N_PIPE
    for section_index in reversed(range(N_PIPE)):
        counts_here = token_counts[section_index].reshape(REPL, MB).T
        live_rows = (positions[None, None, :] < counts_here[:, :, None]).reshape(MB, TOKENS)
        masked = jnp.where(live_rows[:, :, None], key_grads[section_index], jnp.zeros_like(key_grads[section_index]))
        weight_half = master_weight[section_index].astype(jnp.bfloat16)
        terms = jnp.einsum('mtk,rk->mtr', masked.astype(jnp.float32), weight_half.astype(jnp.float32), precision=lax.Precision.HIGHEST)
        result = (incoming.astype(jnp.float32) + terms).astype(jnp.bfloat16)
        grad_list[section_index] = result
        incoming = result
        gradient = lax.dot_general(layer_inputs[section_index].reshape(MB * TOKENS, D), masked.reshape(MB * TOKENS, KV), (((0,), (0,)), ((), ())), preferred_element_type=jnp.float32) / loss_scale
        updated = adamw_update(master_weight[section_index], first_moment[section_index], second_moment[section_index], gradient)
        weight_list[section_index] = updated[0]
        first_list[section_index] = updated[1]
        second_list[section_index] = updated[2]
    return (jnp.stack(grad_list), jnp.stack(weight_list), jnp.stack(first_list), jnp.stack(second_list))
```

```python
import functools

import jax
import jax.numpy as jnp
from jax import lax
from jax.experimental import pallas as pl
from jax.experimental.pallas import tpu as pltpu
from jax.sharding import PartitionSpec as P

beta_one = 0.9
beta_two = 0.95
learn_rate = 0.01
decay_rate = 0.1
adam_eps = 1e-08
loss_scale = 256.0
first_bias = 1.0 - 0.9**10
second_bias = 1.0 - 0.95**10

MESH = pl.DeviceIdType.MESH
COLS = 128


def adamw_update(weight_part, first_part, second_part, gradient):
    first_next = beta_one * first_part + (1.0 - beta_one) * gradient
    second_next = beta_two * second_part + (1.0 - beta_two) * gradient * gradient
    first_hat = first_next / first_bias
    second_hat = second_next / second_bias
    weight_next = weight_part - learn_rate * (
        first_hat / (jnp.sqrt(second_hat) + adam_eps) + decay_rate * weight_part
    )
    return (weight_next, first_next, second_next)


def kernel(
    n_pipe, n_dp, n_fsdp,
    counts, x_hbm, k_hbm, w_hbm,
    out_hbm, grad_hbm,
    x, k, km, wstage, wfull, inc, res, mine, psend, precv, ysend, yrecv, xsend, xrecv, grad,
    load_sem, chain_send, chain_recv, out_sem,
    w_send, w_recv, wf_send, wf_recv,
    p_send, p_recv, y_send, y_recv, x_send, x_recv, g_send, g_recv, grad_sem,
):
    micro, tokens, _ = x.shape
    width = k.shape[-1]
    rows = w_hbm.shape[1]
    half = rows // 2
    per_shard = micro * (rows // COLS)
    n_chunks = n_fsdp * per_shard
    per_half = half // COLS
    n_pieces = n_fsdp * per_half

    s = lax.axis_index("pipe")
    d = lax.axis_index("dp")
    f = lax.axis_index("fsdp")
    core = lax.rem(d, 2)
    core_peer = d + 1 - 2 * core
    far_peer = lax.rem(d + 2, n_dp)

    def remote(src, dst, send, recv, **where):
        return pltpu.make_async_remote_copy(
            src_ref=src, dst_ref=dst, send_sem=send, recv_sem=recv,
            device_id=where, device_id_type=MESH,
        )

    load_k = pltpu.make_async_copy(k_hbm.at[0], k, load_sem.at[0])
    load_w = pltpu.make_async_copy(w_hbm.at[0], wstage, load_sem.at[1])
    load_x = pltpu.make_async_copy(x_hbm.at[0], x, load_sem.at[2])
    load_k.start()
    load_w.start()
    load_x.start()

    barrier = pltpu.get_barrier_semaphore()
    pl.semaphore_signal(barrier, inc=1, device_id={"dp": core_peer}, device_id_type=MESH)
    pl.semaphore_signal(barrier, inc=1, device_id={"dp": far_peer}, device_id_type=MESH)
    for i in range(1, n_fsdp):
        pl.semaphore_signal(
            barrier, inc=1, device_id={"fsdp": lax.rem(f + i, n_fsdp)}, device_id_type=MESH
        )

    @pl.when(s > 0)
    def _():
        pl.semaphore_signal(barrier, inc=1, device_id={"pipe": s - 1}, device_id_type=MESH)

    @pl.when(s < n_pipe - 1)
    def _():
        pl.semaphore_signal(barrier, inc=1, device_id={"pipe": s + 1}, device_id_type=MESH)

    load_k.wait()
    for m in range(micro):
        live = lax.broadcasted_iota(jnp.int32, (tokens, width), 0) < counts[0, m]
        km[m * tokens:(m + 1) * tokens, :] = jnp.where(live, k[m], jnp.zeros_like(k[m]))
    load_w.wait()

    def convert(i, _):
        at = pl.ds(pl.multiple_of(i * COLS, COLS), COLS)
        wfull[f, at, :] = wstage[at, :].astype(jnp.bfloat16)
        return 0

    lax.fori_loop(0, rows // COLS, convert, 0)

    neighbours = n_fsdp + 1 + jnp.minimum(s, 1) + jnp.minimum(n_pipe - 1 - s, 1)
    pl.semaphore_wait(barrier, neighbours)

    my_half = pl.ds(pl.multiple_of(core * half, half), half)

    def w_copy(i):
        return remote(
            wfull.at[f, my_half], wfull.at[f, my_half], w_send.at[i - 1], w_recv.at[i - 1],
            fsdp=lax.rem(f + i, n_fsdp),
        )

    def w_forward(i):
        source = lax.rem(f + n_fsdp - i, n_fsdp)
        return remote(
            wfull.at[source, my_half], wfull.at[source, my_half],
            wf_send.at[i - 1], wf_recv.at[i - 1], dp=core_peer,
        )

    for i in range(1, n_fsdp):
        w_copy(i).start()
    load_x.wait()

    def chain_copy(j):
        return remote(res.at[j], inc.at[j], chain_send.at[j], chain_recv.at[j], pipe=s - 1)

    def place(j):
        shard = lax.rem(f + j // per_shard, n_fsdp)
        within = lax.rem(j, per_shard)
        return shard, within // micro, lax.rem(within, micro)

    def out_copy(j):
        shard, block, m = place(j)
        at = pl.ds(pl.multiple_of(shard * rows + block * COLS, COLS), COLS)
        return pltpu.make_async_copy(res.at[j], out_hbm.at[0, m, :, at], out_sem.at[j])

    def chain_step(j):
        shard, block, m = place(j)
        w_block = wfull[shard, pl.ds(pl.multiple_of(block * COLS, COLS), COLS), :]
        k_block = km[pl.ds(pl.multiple_of(m * tokens, tokens), tokens), :]
        term = lax.dot_general(
            k_block, w_block, (((1,), (1,)), ((), ())), preferred_element_type=jnp.float32
        )

        @pl.when(s < n_pipe - 1)
        def _():
            chain_copy(j).wait_recv()
            res[j] = (inc[j].astype(jnp.float32) + term).astype(jnp.bfloat16)

        @pl.when(s == n_pipe - 1)
        def _():
            res[j] = term.astype(jnp.bfloat16)

        @pl.when(s > 0)
        def _():
            chain_copy(j).start()

        out_copy(j).start()

    def piece_at(q):
        return q // per_half, pl.ds(pl.multiple_of(lax.rem(q, per_half) * COLS, COLS), COLS)

    def product(q, which):
        shard = q // per_half
        start = shard * rows + which * half + lax.rem(q, per_half) * COLS
        x_block = x[:, :, pl.ds(pl.multiple_of(start, COLS), COLS)].reshape(micro * tokens, COLS)
        return lax.dot_general(
            x_block, km[...], (((0,), (0,)), ((), ())), preferred_element_type=jnp.float32
        )

    def piece_copy(q):
        shard, at = piece_at(q)
        return remote(
            psend.at[shard, at], precv.at[shard, at], p_send.at[q], p_recv.at[q], dp=core_peer
        )

    def peer_piece(q):
        shard, at = piece_at(q)
        psend[shard, at, :] = product(q, 1 - core).astype(jnp.bfloat16)
        piece_copy(q).start()

    def own_piece(q):
        shard, at = piece_at(q)
        mine[shard, at, :] = product(q, core)

    def y_copy(i):
        return remote(
            ysend.at[i - 1], yrecv.at[i - 1], y_send.at[i - 1], y_recv.at[i - 1],
            fsdp=lax.rem(f + i, n_fsdp),
        )

    x_copy = remote(xsend, xrecv, x_send, x_recv, dp=far_peer)
    g_copy = remote(grad.at[my_half], grad.at[my_half], g_send, g_recv, dp=core_peer)

    def blocks(body):
        def step(b, _):
            body(pl.ds(pl.multiple_of(b * COLS, COLS), COLS), b)
            return 0

        lax.fori_loop(0, per_half, step, 0)

    def sum_pair():
        def wait(q, _):
            piece_copy(q).wait_recv()
            return 0

        lax.fori_loop(0, n_pieces, wait, 0)
        for i in range(1, n_fsdp):
            shard = lax.rem(f + i, n_fsdp)

            def add(at, b, i=i, shard=shard):
                ysend[i - 1, at, :] = (
                    mine[shard, at, :] + precv[shard, at, :].astype(jnp.float32)
                ).astype(jnp.bfloat16)

            blocks(add)
            y_copy(i).start()

    def sum_fsdp():
        for i in range(1, n_fsdp):
            y_copy(i).wait_recv()

        def add(at, b):
            total = mine[f, at, :] + precv[f, at, :].astype(jnp.float32)
            for i in range(1, n_fsdp):
                total = total + yrecv[i - 1, at, :].astype(jnp.float32)
            xsend[at, :] = total.astype(jnp.bfloat16)

        blocks(add)
        x_copy.start()

    def sum_far():
        x_copy.wait_recv()

        def add(at, b):
            to = pl.ds(pl.multiple_of(core * half + b * COLS, COLS), COLS)
            grad[to, :] = (
                xsend[at, :].astype(jnp.float32) + xrecv[at, :].astype(jnp.float32)
            ) / loss_scale

        blocks(add)
        g_copy.start()

    def forward_weights():
        for i in range(1, n_fsdp):
            w_copy(i).wait_recv()
            w_forward(i).start()

    def weights_here():
        for i in range(1, n_fsdp):
            w_forward(i).wait_recv()

    steps_a = n_pieces // 2

    def run(first, last):
        def step(j, _):
            chain_step(j)
            if last <= steps_a:
                peer_piece(2 * j)
                peer_piece(2 * j + 1)
            elif last <= 2 * steps_a:
                own_piece(2 * (j - steps_a))
                own_piece(2 * (j - steps_a) + 1)
            return 0

        if last > first:
            lax.fori_loop(first, last, step, 0)

    events = [
        (min(20, per_shard - 1), forward_weights),
        (per_shard, weights_here),
        (steps_a, None),
        (2 * steps_a, None),
        (2 * steps_a + 2, sum_pair),
        (44, sum_fsdp),
        (60, sum_far),
    ]
    done = 0
    for when, event in sorted(events, key=lambda pair: pair[0]):
        run(done, when)
        done = when
        if event is not None:
            event()
    run(done, n_chunks)

    g_copy.wait_recv()
    store_grad = pltpu.make_async_copy(grad, grad_hbm.at[0], grad_sem)
    store_grad.start()

    def finish(j, _):
        @pl.when(s > 0)
        def _():
            chain_copy(j).wait_send()

        out_copy(j).wait()
        return 0

    lax.fori_loop(0, n_chunks, finish, 0)

    def finish_pieces(q, _):
        piece_copy(q).wait_send()
        return 0

    lax.fori_loop(0, n_pieces, finish_pieces, 0)
    for i in range(1, n_fsdp):
        w_copy(i).wait_send()
        w_forward(i).wait_send()
        y_copy(i).wait_send()
    x_copy.wait_send()
    g_copy.wait_send()
    store_grad.wait()


def local(mesh, layer_inputs, key_grads, token_counts, master_weight, first_moment, second_moment):
    n_pipe, n_dp, n_fsdp = (mesh.shape[name] for name in ("pipe", "dp", "fsdp"))
    _, micro, tokens, features = layer_inputs.shape
    width = key_grads.shape[-1]
    rows = master_weight.shape[1]
    half = rows // 2
    n_chunks = micro * features // COLS
    n_pieces = n_fsdp * half // COLS
    others = n_fsdp - 1
    half_bf = (half, width)
    bf, f32 = jnp.bfloat16, jnp.float32
    dma = pltpu.SemaphoreType.DMA
    anywhere = pl.BlockSpec(memory_space=pl.ANY)
    input_grads, gradient = pl.pallas_call(
        functools.partial(kernel, n_pipe, n_dp, n_fsdp),
        out_shape=(
            jax.ShapeDtypeStruct(layer_inputs.shape, bf),
            jax.ShapeDtypeStruct(master_weight.shape, f32),
        ),
        in_specs=[pl.BlockSpec(memory_space=pltpu.SMEM), anywhere, anywhere, anywhere],
        out_specs=(anywhere, anywhere),
        scratch_shapes=[
            pltpu.VMEM((micro, tokens, features), bf),
            pltpu.VMEM((micro, tokens, width), bf),
            pltpu.VMEM((micro * tokens, width), bf),
            pltpu.VMEM((rows, width), f32),
            pltpu.VMEM((n_fsdp, rows, width), bf),
            pltpu.VMEM((n_chunks, tokens, COLS), bf),
            pltpu.VMEM((n_chunks, tokens, COLS), bf),
            pltpu.VMEM((n_fsdp,) + half_bf, f32),
            pltpu.VMEM((n_fsdp,) + half_bf, bf),
            pltpu.VMEM((n_fsdp,) + half_bf, bf),
            pltpu.VMEM((others,) + half_bf, bf),
            pltpu.VMEM((others,) + half_bf, bf),
            pltpu.VMEM(half_bf, bf),
            pltpu.VMEM(half_bf, bf),
            pltpu.VMEM((rows, width), f32),
            dma((3,)),
            dma((n_chunks,)), dma((n_chunks,)), dma((n_chunks,)),
            dma((others,)), dma((others,)), dma((others,)), dma((others,)),
            dma((n_pieces,)), dma((n_pieces,)),
            dma((others,)), dma((others,)),
            dma, dma, dma, dma, dma,
        ],
        compiler_params=pltpu.CompilerParams(
            collective_id=0, has_side_effects=True, vmem_limit_bytes=48 * 1024 * 1024
        ),
        cost_estimate=pl.CostEstimate(
            flops=4 * micro * tokens * width * features,
            bytes_accessed=32 * 1024 * 1024,
            transcendentals=0,
        ),
    )(token_counts, layer_inputs, key_grads, master_weight)
    new_weight, new_first, new_second = adamw_update(
        master_weight, first_moment, second_moment, gradient
    )
    return (input_grads, new_weight, new_first, new_second)


def solution(mesh):
    in_specs = (
        P("pipe", None, ("dp", "fsdp"), None),
        P("pipe", None, ("dp", "fsdp"), None),
        P("pipe", ("dp", "fsdp")),
        P("pipe", "fsdp", None),
        P("pipe", "fsdp", None),
        P("pipe", "fsdp", None),
    )
    out_specs = (
        P("pipe", None, ("dp", "fsdp"), None),
        P("pipe", "fsdp", None),
        P("pipe", "fsdp", None),
        P("pipe", "fsdp", None),
    )
    return jax.shard_map(
        functools.partial(local, mesh), mesh=mesh, in_specs=in_specs, out_specs=out_specs,
        check_vma=False,
    )
```

```python
import functools

import jax
import jax.numpy as jnp
from jax import lax
from jax.experimental import pallas as pl
from jax.experimental.pallas import tpu as pltpu
from jax.sharding import PartitionSpec as P

beta_one = 0.9
beta_two = 0.95
learn_rate = 0.01
decay_rate = 0.1
adam_eps = 1e-08
loss_scale = 256.0
first_bias = 1.0 - 0.9**10
second_bias = 1.0 - 0.95**10

MESH = pl.DeviceIdType.MESH
IN_FLIGHT = 4
COLS = 128


def adamw_update(weight_part, first_part, second_part, gradient):
    first_next = beta_one * first_part + (1.0 - beta_one) * gradient
    second_next = beta_two * second_part + (1.0 - beta_two) * gradient * gradient
    first_hat = first_next / first_bias
    second_hat = second_next / second_bias
    weight_next = weight_part - learn_rate * (
        first_hat / (jnp.sqrt(second_hat) + adam_eps) + decay_rate * weight_part
    )
    return (weight_next, first_next, second_next)


def kernel(
    n_pipe, n_dp, n_fsdp,
    counts_hbm, x_hbm, k_hbm, w_hbm,
    out_hbm, grad_hbm,
    counts, x, k, km, wstage, wfull, inc, res, mine, psend, precv, ysend, yrecv, xsend, xrecv,
    load_sem, chain_send, chain_recv, out_sem,
    w_send, w_recv, wf_send, wf_recv,
    p_send, p_recv, y_send, y_recv, x_send, x_recv, g_send, g_recv, grad_sem,
):
    micro, tokens, _ = x.shape
    width = k.shape[-1]
    rows = w_hbm.shape[1]
    half = rows // 2
    grad = wstage
    per_shard = micro * (rows // COLS)
    n_chunks = n_fsdp * per_shard
    per_half = half // COLS
    n_pieces = n_fsdp * per_half

    s = lax.axis_index("pipe")
    d = lax.axis_index("dp")
    f = lax.axis_index("fsdp")
    core = lax.rem(d, 2)
    core_peer = d + 1 - 2 * core
    far_peer = lax.rem(d + 2, n_dp)

    def remote(src, dst, send, recv, **where):
        return pltpu.make_async_remote_copy(
            src_ref=src, dst_ref=dst, send_sem=send, recv_sem=recv,
            device_id=where, device_id_type=MESH,
        )

    load_k = pltpu.make_async_copy(k_hbm.at[0], k, load_sem.at[0])
    load_counts = pltpu.make_async_copy(counts_hbm, counts, load_sem.at[3])
    lead, rest = pl.ds(0, COLS), pl.ds(COLS, rows - COLS)
    load_lead = pltpu.make_async_copy(w_hbm.at[0, lead], wstage.at[lead], load_sem.at[1])
    load_rest = pltpu.make_async_copy(w_hbm.at[0, rest], wstage.at[rest], load_sem.at[4])
    load_x = pltpu.make_async_copy(x_hbm.at[0], x, load_sem.at[2])
    load_counts.start()
    load_k.start()
    load_lead.start()
    load_rest.start()
    load_x.start()

    barrier = pltpu.get_barrier_semaphore()
    pl.semaphore_signal(barrier, inc=1, device_id={"dp": core_peer}, device_id_type=MESH)
    pl.semaphore_signal(barrier, inc=1, device_id={"dp": far_peer}, device_id_type=MESH)
    for i in range(1, n_fsdp):
        pl.semaphore_signal(
            barrier, inc=1, device_id={"fsdp": lax.rem(f + i, n_fsdp)}, device_id_type=MESH
        )

    @pl.when(s > 0)
    def _():
        pl.semaphore_signal(barrier, inc=1, device_id={"pipe": s - 1}, device_id_type=MESH)

    @pl.when(s < n_pipe - 1)
    def _():
        pl.semaphore_signal(barrier, inc=1, device_id={"pipe": s + 1}, device_id_type=MESH)

    load_counts.wait()
    load_k.wait()
    for m in range(micro):
        live = lax.broadcasted_iota(jnp.int32, (tokens, width), 0) < counts[0, m]
        km[m * tokens:(m + 1) * tokens, :] = jnp.where(live, k[m], jnp.zeros_like(k[m]))
    load_lead.wait()
    wfull[f, lead, :] = wstage[lead, :].astype(jnp.bfloat16)

    neighbours = n_fsdp + 1 + jnp.minimum(s, 1) + jnp.minimum(n_pipe - 1 - s, 1)
    pl.semaphore_wait(barrier, neighbours)

    my_half = pl.ds(pl.multiple_of(core * half, half), half)

    def w_copy(i):
        return remote(
            wfull.at[f, my_half], wfull.at[f, my_half], w_send.at[i - 1], w_recv.at[i - 1],
            fsdp=lax.rem(f + i, n_fsdp),
        )

    def w_forward(i):
        source = lax.rem(f + n_fsdp - i, n_fsdp)
        return remote(
            wfull.at[source, my_half], wfull.at[source, my_half],
            wf_send.at[i - 1], wf_recv.at[i - 1], dp=core_peer,
        )

    def chain_copy(j):
        return remote(res.at[j], inc.at[j], chain_send.at[j], chain_recv.at[j], pipe=s - 1)

    def place(j):
        shard = lax.rem(f + j // per_shard, n_fsdp)
        within = lax.rem(j, per_shard)
        return shard, within // micro, lax.rem(within, micro)

    def out_copy(j):
        shard, block, m = place(j)
        at = pl.ds(pl.multiple_of(shard * rows + block * COLS, COLS), COLS)
        return pltpu.make_async_copy(res.at[j], out_hbm.at[0, m, :, at], out_sem.at[j])

    def chain_step(j):
        shard, block, m = place(j)
        w_block = wfull[shard, pl.ds(pl.multiple_of(block * COLS, COLS), COLS), :]
        k_block = km[pl.ds(pl.multiple_of(m * tokens, tokens), tokens), :]
        term = lax.dot_general(
            k_block, w_block, (((1,), (1,)), ((), ())), preferred_element_type=jnp.float32
        )

        @pl.when(s < n_pipe - 1)
        def _():
            chain_copy(j).wait_recv()
            res[j] = (inc[j].astype(jnp.float32) + term).astype(jnp.bfloat16)

        @pl.when(s == n_pipe - 1)
        def _():
            res[j] = term.astype(jnp.bfloat16)

        @pl.when(s > 0)
        def _():
            chain_copy(j).start()

        out_copy(j).start()

    def chain_done(j):
        @pl.when(s > 0)
        def _():
            chain_copy(j).wait_send()

        out_copy(j).wait()

    def piece_at(q):
        return q // per_half, pl.ds(pl.multiple_of(lax.rem(q, per_half) * COLS, COLS), COLS)

    def product(q, which):
        shard = q // per_half
        start = shard * rows + which * half + lax.rem(q, per_half) * COLS
        x_block = x[:, :, pl.ds(pl.multiple_of(start, COLS), COLS)].reshape(micro * tokens, COLS)
        return lax.dot_general(
            x_block, km[...], (((0,), (0,)), ((), ())), preferred_element_type=jnp.float32
        )

    def piece_copy(q):
        shard, at = piece_at(q)
        return remote(
            psend.at[shard, at], precv.at[shard, at], p_send.at[q], p_recv.at[q], dp=core_peer
        )

    def peer_piece(q):
        shard, at = piece_at(q)
        psend[shard, at, :] = product(q, 1 - core).astype(jnp.bfloat16)
        piece_copy(q).start()

    def own_piece(q):
        shard, at = piece_at(q)
        mine[shard, at, :] = product(q, core)

    def y_copy(i):
        return remote(
            ysend.at[i - 1], yrecv.at[i - 1], y_send.at[i - 1], y_recv.at[i - 1],
            fsdp=lax.rem(f + i, n_fsdp),
        )

    x_copy = remote(xsend, xrecv, x_send, x_recv, dp=far_peer)
    g_copy = remote(grad.at[my_half], grad.at[my_half], g_send, g_recv, dp=core_peer)

    def blocks(body):
        def step(b, _):
            body(pl.ds(pl.multiple_of(b * COLS, COLS), COLS), b)
            return 0

        lax.fori_loop(0, per_half, step, 0)

    def sum_pair():
        def wait(q, _):
            piece_copy(q).wait_recv()
            return 0

        lax.fori_loop(0, n_pieces, wait, 0)
        for i in range(1, n_fsdp):
            shard = lax.rem(f + i, n_fsdp)

            def add(at, b, i=i, shard=shard):
                ysend[i - 1, at, :] = (
                    mine[shard, at, :] + precv[shard, at, :].astype(jnp.float32)
                ).astype(jnp.bfloat16)

            blocks(add)
            y_copy(i).start()

    def sum_fsdp():
        for i in range(1, n_fsdp):
            y_copy(i).wait_recv()

        def add(at, b):
            total = mine[f, at, :] + precv[f, at, :].astype(jnp.float32)
            for i in range(1, n_fsdp):
                total = total + yrecv[i - 1, at, :].astype(jnp.float32)
            xsend[at, :] = total.astype(jnp.bfloat16)

        blocks(add)
        x_copy.start()

    def sum_far():
        x_copy.wait_recv()

        def add(at, b):
            to = pl.ds(pl.multiple_of(core * half + b * COLS, COLS), COLS)
            grad[to, :] = (
                xsend[at, :].astype(jnp.float32) + xrecv[at, :].astype(jnp.float32)
            ) / loss_scale

        blocks(add)
        g_copy.start()

        def finish_pieces(q, _):
            piece_copy(q).wait_send()
            return 0

        lax.fori_loop(0, n_pieces, finish_pieces, 0)
        for i in range(1, n_fsdp):
            w_copy(i).wait_send()
            w_forward(i).wait_send()
            y_copy(i).wait_send()
        x_copy.wait_send()

    store_grad = pltpu.make_async_copy(grad, grad_hbm.at[0], grad_sem)

    def gradient_here():
        g_copy.wait_recv()
        g_copy.wait_send()
        store_grad.start()

    def forward_weights():
        for i in range(1, n_fsdp):
            w_copy(i).wait_recv()
            w_forward(i).start()

    def weights_here():
        for i in range(1, n_fsdp):
            w_forward(i).wait_recv()

    steps_a = n_pieces // 2

    def run(first, last):
        def step(j, _):
            @pl.when(j >= IN_FLIGHT)
            def _():
                chain_done(j - IN_FLIGHT)

            @pl.when(jnp.logical_or(s < n_pipe - 1, j >= micro))
            def _():
                chain_step(j)

            if last <= steps_a:
                peer_piece(2 * j)
                peer_piece(2 * j + 1)
            elif last <= 2 * steps_a:
                own_piece(2 * (j - steps_a))
                own_piece(2 * (j - steps_a) + 1)
            return 0

        if last > first:
            lax.fori_loop(first, last, step, 0)

    events = [
        (min(20, per_shard - 1), forward_weights),
        (per_shard, weights_here),
        (steps_a, None),
        (2 * steps_a, None),
        (2 * steps_a + 1, sum_pair),
        (9 * n_chunks // 16, sum_fsdp),
        (27 * n_chunks // 32, sum_far),
        (31 * n_chunks // 32, gradient_here),
    ]

    @pl.when(s == n_pipe - 1)
    def _():
        for j in range(micro):
            chain_step(j)

    load_rest.wait()

    def convert(i, _):
        at = pl.ds(pl.multiple_of(i * COLS, COLS), COLS)
        wfull[f, at, :] = wstage[at, :].astype(jnp.bfloat16)
        return 0

    lax.fori_loop(1, rows // COLS, convert, 0)
    for i in range(1, n_fsdp):
        w_copy(i).start()
    load_x.wait()
    done = 0
    for when, event in sorted(events, key=lambda pair: pair[0]):
        run(done, when)
        done = when
        if event is not None:
            event()
    run(done, n_chunks)

    for j in range(max(n_chunks - IN_FLIGHT, 0), n_chunks):
        chain_done(j)
    store_grad.wait()


def local(mesh, layer_inputs, key_grads, token_counts, master_weight, first_moment, second_moment):
    n_pipe, n_dp, n_fsdp = (mesh.shape[name] for name in ("pipe", "dp", "fsdp"))
    _, micro, tokens, features = layer_inputs.shape
    width = key_grads.shape[-1]
    rows = master_weight.shape[1]
    half = rows // 2
    n_chunks = micro * features // COLS
    n_pieces = n_fsdp * half // COLS
    others = n_fsdp - 1
    half_bf = (half, width)
    bf, f32 = jnp.bfloat16, jnp.float32
    dma = pltpu.SemaphoreType.DMA
    anywhere = pl.BlockSpec(memory_space=pl.ANY)
    input_grads, gradient = pl.pallas_call(
        functools.partial(kernel, n_pipe, n_dp, n_fsdp),
        out_shape=(
            jax.ShapeDtypeStruct(layer_inputs.shape, bf),
            jax.ShapeDtypeStruct(master_weight.shape, f32),
        ),
        in_specs=[pl.BlockSpec(memory_space=pltpu.HBM)] * 4,
        out_specs=(anywhere, anywhere),
        scratch_shapes=[
            pltpu.SMEM(token_counts.shape, jnp.int32),
            pltpu.VMEM((micro, tokens, features), bf),
            pltpu.VMEM((micro, tokens, width), bf),
            pltpu.VMEM((micro * tokens, width), bf),
            pltpu.VMEM((rows, width), f32),
            pltpu.VMEM((n_fsdp, rows, width), bf),
            pltpu.VMEM((n_chunks, tokens, COLS), bf),
            pltpu.VMEM((n_chunks, tokens, COLS), bf),
            pltpu.VMEM((n_fsdp,) + half_bf, f32),
            pltpu.VMEM((n_fsdp,) + half_bf, bf),
            pltpu.VMEM((n_fsdp,) + half_bf, bf),
            pltpu.VMEM((others,) + half_bf, bf),
            pltpu.VMEM((others,) + half_bf, bf),
            pltpu.VMEM(half_bf, bf),
            pltpu.VMEM(half_bf, bf),
            dma((5,)),
            dma((n_chunks,)), dma((n_chunks,)), dma((n_chunks,)),
            dma((others,)), dma((others,)), dma((others,)), dma((others,)),
            dma((n_pieces,)), dma((n_pieces,)),
            dma((others,)), dma((others,)),
            dma, dma, dma, dma, dma,
        ],
        compiler_params=pltpu.CompilerParams(
            collective_id=0, has_side_effects=True, vmem_limit_bytes=36 * 1024 * 1024
        ),
        cost_estimate=pl.CostEstimate(
            flops=4 * micro * tokens * width * features,
            bytes_accessed=32 * 1024 * 1024,
            transcendentals=0,
        ),
    )(
        *[
            pltpu.with_memory_space_constraint(array, pltpu.HBM)
            for array in (token_counts, layer_inputs, key_grads, master_weight)
        ]
    )
    new_weight, new_first, new_second = adamw_update(
        master_weight, first_moment, second_moment, gradient
    )
    return (input_grads, new_weight, new_first, new_second)


def solution(mesh):
    in_specs = (
        P("pipe", None, ("dp", "fsdp"), None),
        P("pipe", None, ("dp", "fsdp"), None),
        P("pipe", ("dp", "fsdp")),
        P("pipe", "fsdp", None),
        P("pipe", "fsdp", None),
        P("pipe", "fsdp", None),
    )
    out_specs = (
        P("pipe", None, ("dp", "fsdp"), None),
        P("pipe", "fsdp", None),
        P("pipe", "fsdp", None),
        P("pipe", "fsdp", None),
    )
    return jax.shard_map(
        functools.partial(local, mesh), mesh=mesh, in_specs=in_specs, out_specs=out_specs,
        check_vma=False,
    )
```

```python
import functools

import jax
import jax.numpy as jnp
from jax import lax
from jax.experimental import pallas as pl
from jax.experimental.pallas import tpu as pltpu
from jax.sharding import PartitionSpec as P

beta_one = 0.9
beta_two = 0.95
learn_rate = 0.01
decay_rate = 0.1
adam_eps = 1e-08
loss_scale = 256.0
first_bias = 1.0 - 0.9**10
second_bias = 1.0 - 0.95**10

MESH = pl.DeviceIdType.MESH
IN_FLIGHT = 4
COLS = 128


def adamw_update(weight_part, first_part, second_part, gradient):
    first_next = beta_one * first_part + (1.0 - beta_one) * gradient
    second_next = beta_two * second_part + (1.0 - beta_two) * gradient * gradient
    first_hat = first_next / first_bias
    second_hat = second_next / second_bias
    weight_next = weight_part - learn_rate * (
        first_hat / (jnp.sqrt(second_hat) + adam_eps) + decay_rate * weight_part
    )
    return (weight_next, first_next, second_next)


def kernel(
    n_pipe, n_dp, n_fsdp,
    counts_hbm, x_hbm, k_hbm, w_hbm,
    out_hbm, grad_hbm,
    counts, x, k, km, wstage, wfull, inc, res, mine, psend, precv, ysend, yrecv, xsend, xrecv,
    load_sem, chain_send, chain_recv, out_sem,
    w_send, w_recv, wf_send, wf_recv,
    p_send, p_recv, y_send, y_recv, x_send, x_recv, g_send, g_recv, grad_sem,
):
    micro, tokens, _ = x.shape
    width = k.shape[-1]
    rows = w_hbm.shape[1]
    half = rows // 2
    grad = wstage
    per_shard = micro * (rows // COLS)
    n_chunks = n_fsdp * per_shard
    per_half = half // COLS
    n_pieces = n_fsdp * per_half

    s = lax.axis_index("pipe")
    d = lax.axis_index("dp")
    f = lax.axis_index("fsdp")
    core = lax.rem(d, 2)
    core_peer = d + 1 - 2 * core
    far_peer = lax.rem(d + 2, n_dp)

    def remote(src, dst, send, recv, **where):
        return pltpu.make_async_remote_copy(
            src_ref=src, dst_ref=dst, send_sem=send, recv_sem=recv,
            device_id=where, device_id_type=MESH,
        )

    load_k = pltpu.make_async_copy(k_hbm.at[0], k, load_sem.at[0])
    load_counts = pltpu.make_async_copy(counts_hbm, counts, load_sem.at[3])
    lead, rest = pl.ds(0, COLS), pl.ds(COLS, rows - COLS)
    load_lead = pltpu.make_async_copy(w_hbm.at[0, lead], wstage.at[lead], load_sem.at[1])
    load_rest = pltpu.make_async_copy(w_hbm.at[0, rest], wstage.at[rest], load_sem.at[4])
    load_x = pltpu.make_async_copy(x_hbm.at[0], x, load_sem.at[2])
    load_counts.start()
    load_k.start()
    load_lead.start()
    load_rest.start()
    load_x.start()

    barrier = pltpu.get_barrier_semaphore()
    pl.semaphore_signal(barrier, inc=1, device_id={"dp": core_peer}, device_id_type=MESH)
    pl.semaphore_signal(barrier, inc=1, device_id={"dp": far_peer}, device_id_type=MESH)
    for i in range(1, n_fsdp):
        pl.semaphore_signal(
            barrier, inc=1, device_id={"fsdp": lax.rem(f + i, n_fsdp)}, device_id_type=MESH
        )

    @pl.when(s > 0)
    def _():
        pl.semaphore_signal(barrier, inc=1, device_id={"pipe": s - 1}, device_id_type=MESH)

    @pl.when(s < n_pipe - 1)
    def _():
        pl.semaphore_signal(barrier, inc=1, device_id={"pipe": s + 1}, device_id_type=MESH)

    load_counts.wait()
    load_k.wait()
    for m in range(micro):
        live = lax.broadcasted_iota(jnp.int32, (tokens, width), 0) < counts[0, m]
        km[m * tokens:(m + 1) * tokens, :] = jnp.where(live, k[m], jnp.zeros_like(k[m]))
    load_lead.wait()
    wfull[f, lead, :] = wstage[lead, :].astype(jnp.bfloat16)

    neighbours = n_fsdp + 1 + jnp.minimum(s, 1) + jnp.minimum(n_pipe - 1 - s, 1)
    pl.semaphore_wait(barrier, neighbours)

    my_half = pl.ds(pl.multiple_of(core * half, half), half)

    def w_copy(i):
        return remote(
            wfull.at[f, my_half], wfull.at[f, my_half], w_send.at[i - 1], w_recv.at[i - 1],
            fsdp=lax.rem(f + i, n_fsdp),
        )

    def w_forward(i):
        source = lax.rem(f + n_fsdp - i, n_fsdp)
        return remote(
            wfull.at[source, my_half], wfull.at[source, my_half],
            wf_send.at[i - 1], wf_recv.at[i - 1], dp=core_peer,
        )

    def chain_copy(j):
        return remote(res.at[j], inc.at[j], chain_send.at[j], chain_recv.at[j], pipe=s - 1)

    def place(j):
        shard = lax.rem(f + j // per_shard, n_fsdp)
        within = lax.rem(j, per_shard)
        return shard, within // micro, lax.rem(within, micro)

    def out_copy(j):
        shard, block, m = place(j)
        at = pl.ds(pl.multiple_of(shard * rows + block * COLS, COLS), COLS)
        return pltpu.make_async_copy(res.at[j], out_hbm.at[0, m, :, at], out_sem.at[j])

    def chain_step(j):
        shard, block, m = place(j)
        w_block = wfull[shard, pl.ds(pl.multiple_of(block * COLS, COLS), COLS), :]
        k_block = km[pl.ds(pl.multiple_of(m * tokens, tokens), tokens), :]
        term = lax.dot_general(
            k_block, w_block, (((1,), (1,)), ((), ())), preferred_element_type=jnp.float32
        )

        @pl.when(s < n_pipe - 1)
        def _():
            chain_copy(j).wait_recv()
            res[j] = (inc[j].astype(jnp.float32) + term).astype(jnp.bfloat16)

        @pl.when(s == n_pipe - 1)
        def _():
            res[j] = term.astype(jnp.bfloat16)

        @pl.when(s > 0)
        def _():
            chain_copy(j).start()

        out_copy(j).start()

    def chain_done(j):
        @pl.when(s > 0)
        def _():
            chain_copy(j).wait_send()

        out_copy(j).wait()

    def piece_at(q):
        shard = lax.rem(f + 1 + q // per_half, n_fsdp)
        return shard, pl.ds(pl.multiple_of(lax.rem(q, per_half) * COLS, COLS), COLS)

    def block_at(b):
        return pl.ds(pl.multiple_of(b * COLS, COLS), COLS)

    def product(q, which):
        shard, _ = piece_at(q)
        start = shard * rows + which * half + lax.rem(q, per_half) * COLS
        x_block = x[:, :, pl.ds(pl.multiple_of(start, COLS), COLS)].reshape(micro * tokens, COLS)
        return lax.dot_general(
            x_block, km[...], (((0,), (0,)), ((), ())), preferred_element_type=jnp.float32
        )

    def piece_copy(q):
        shard, at = piece_at(q)
        return remote(
            psend.at[shard, at], precv.at[shard, at], p_send.at[q], p_recv.at[q], dp=core_peer
        )

    def peer_piece(q):
        shard, at = piece_at(q)
        psend[shard, at, :] = product(q, 1 - core).astype(jnp.bfloat16)
        piece_copy(q).start()

    def peer_pieces(t):
        peer_piece(2 * t)
        peer_piece(2 * t + 1)

    def pair_sum(q):
        shard, at = piece_at(q)
        term = product(q, core)
        piece_copy(q).wait_recv()
        return term + precv[shard, at, :].astype(jnp.float32)

    def y_copy(q):
        i, at = q // per_half, block_at(lax.rem(q, per_half))
        return remote(
            ysend.at[i, at], yrecv.at[i, at], y_send.at[q], y_recv.at[q],
            fsdp=lax.rem(f + 1 + i, n_fsdp),
        )

    def others_piece(q):
        ysend[q // per_half, block_at(lax.rem(q, per_half)), :] = pair_sum(q).astype(jnp.bfloat16)
        y_copy(q).start()

    n_others = (n_fsdp - 1) * per_half

    def own_piece(b):
        mine[block_at(b), :] = pair_sum(n_others + b)

    def x_copy(b):
        at = block_at(b)
        return remote(xsend.at[at], xrecv.at[at], x_send.at[b], x_recv.at[b], dp=far_peer)

    def g_copy(b):
        at = block_at(core * per_half + b)
        return remote(grad.at[at], grad.at[at], g_send.at[b], g_recv.at[b], dp=core_peer)

    def sum_fsdp(b):
        at = block_at(b)
        total = mine[at, :]
        for i in range(n_fsdp - 1):
            y_copy(i * per_half + b).wait_recv()
            total = total + yrecv[i, at, :].astype(jnp.float32)
        xsend[at, :] = total.astype(jnp.bfloat16)
        x_copy(b).start()

    def sum_far(b):
        at = block_at(b)
        x_copy(b).wait_recv()
        grad[block_at(core * per_half + b), :] = (
            xsend[at, :].astype(jnp.float32) + xrecv[at, :].astype(jnp.float32)
        ) / loss_scale
        g_copy(b).start()

    store_grad = pltpu.make_async_copy(grad, grad_hbm.at[0], grad_sem)

    def gradient_here():
        for b in range(per_half):
            g_copy(b).wait_recv()
            g_copy(b).wait_send()
        store_grad.start()

    def finish_pieces():
        def piece(q, _):
            piece_copy(q).wait_send()
            return 0

        lax.fori_loop(0, n_pieces, piece, 0)

    def finish_others():
        for i in range(1, n_fsdp):
            w_copy(i).wait_send()
            w_forward(i).wait_send()

        def piece(q, _):
            y_copy(q).wait_send()
            return 0

        lax.fori_loop(0, n_others, piece, 0)

    def forward_weights():
        for i in range(1, n_fsdp):
            w_copy(i).wait_recv()
            w_forward(i).start()

    def weights_here():
        for i in range(1, n_fsdp):
            w_forward(i).wait_recv()

    works = [
        (0, n_pieces // 2, peer_pieces),
        (n_pieces // 2, n_others, others_piece),
        (n_pieces // 2 + n_others, per_half, own_piece),
        (9 * n_chunks // 16, per_half, sum_fsdp),
        (27 * n_chunks // 32, per_half, sum_far),
    ]

    def run(first, last):
        def step(j, _):
            @pl.when(j >= IN_FLIGHT)
            def _():
                chain_done(j - IN_FLIGHT)

            @pl.when(jnp.logical_or(s < n_pipe - 1, j >= micro))
            def _():
                chain_step(j)

            for start, count, work in works:
                if start <= first and last <= start + count:
                    work(j - start)
            return 0

        if last > first:
            lax.fori_loop(first, last, step, 0)

    events = [
        (min(7 * n_chunks // 16, per_shard - 1), forward_weights),
        (per_shard, weights_here),
        (n_chunks // 2 + 1, finish_pieces),
        (13 * n_chunks // 16, finish_others),
        (63 * n_chunks // 64, gradient_here),
    ]
    for start, count, _ in works:
        events += [(start, None), (start + count, None)]

    @pl.when(s == n_pipe - 1)
    def _():
        for j in range(micro):
            chain_step(j)

    load_rest.wait()

    def convert(i, _):
        at = pl.ds(pl.multiple_of(i * COLS, COLS), COLS)
        wfull[f, at, :] = wstage[at, :].astype(jnp.bfloat16)
        return 0

    lax.fori_loop(1, rows // COLS, convert, 0)
    for i in range(1, n_fsdp):
        w_copy(i).start()
    load_x.wait()
    done = 0
    for when, event in sorted(events, key=lambda pair: pair[0]):
        run(done, when)
        done = when
        if event is not None:
            event()
    run(done, n_chunks)

    for b in range(per_half):
        x_copy(b).wait_send()
    for j in range(max(n_chunks - IN_FLIGHT, 0), n_chunks):
        chain_done(j)
    store_grad.wait()


def local(mesh, layer_inputs, key_grads, token_counts, master_weight, first_moment, second_moment):
    n_pipe, n_dp, n_fsdp = (mesh.shape[name] for name in ("pipe", "dp", "fsdp"))
    _, micro, tokens, features = layer_inputs.shape
    width = key_grads.shape[-1]
    rows = master_weight.shape[1]
    half = rows // 2
    n_chunks = micro * features // COLS
    n_pieces = n_fsdp * half // COLS
    per_half = half // COLS
    others = n_fsdp - 1
    half_bf = (half, width)
    bf, f32 = jnp.bfloat16, jnp.float32
    dma = pltpu.SemaphoreType.DMA
    anywhere = pl.BlockSpec(memory_space=pl.ANY)
    input_grads, gradient = pl.pallas_call(
        functools.partial(kernel, n_pipe, n_dp, n_fsdp),
        out_shape=(
            jax.ShapeDtypeStruct(layer_inputs.shape, bf),
            jax.ShapeDtypeStruct(master_weight.shape, f32),
        ),
        in_specs=[pl.BlockSpec(memory_space=pltpu.HBM)] * 4,
        out_specs=(anywhere, anywhere),
        scratch_shapes=[
            pltpu.SMEM(token_counts.shape, jnp.int32),
            pltpu.VMEM((micro, tokens, features), bf),
            pltpu.VMEM((micro, tokens, width), bf),
            pltpu.VMEM((micro * tokens, width), bf),
            pltpu.VMEM((rows, width), f32),
            pltpu.VMEM((n_fsdp, rows, width), bf),
            pltpu.VMEM((n_chunks, tokens, COLS), bf),
            pltpu.VMEM((n_chunks, tokens, COLS), bf),
            pltpu.VMEM(half_bf, f32),
            pltpu.VMEM((n_fsdp,) + half_bf, bf),
            pltpu.VMEM((n_fsdp,) + half_bf, bf),
            pltpu.VMEM((others,) + half_bf, bf),
            pltpu.VMEM((others,) + half_bf, bf),
            pltpu.VMEM(half_bf, bf),
            pltpu.VMEM(half_bf, bf),
            dma((5,)),
            dma((n_chunks,)), dma((n_chunks,)), dma((n_chunks,)),
            dma((others,)), dma((others,)), dma((others,)), dma((others,)),
            dma((n_pieces,)), dma((n_pieces,)),
            dma((others * per_half,)), dma((others * per_half,)),
            dma((per_half,)), dma((per_half,)), dma((per_half,)), dma((per_half,)), dma,
        ],
        compiler_params=pltpu.CompilerParams(
            collective_id=0, has_side_effects=True, vmem_limit_bytes=36 * 1024 * 1024
        ),
        cost_estimate=pl.CostEstimate(
            flops=4 * micro * tokens * width * features,
            bytes_accessed=32 * 1024 * 1024,
            transcendentals=0,
        ),
    )(
        *[
            pltpu.with_memory_space_constraint(array, pltpu.HBM)
            for array in (token_counts, layer_inputs, key_grads, master_weight)
        ]
    )
    new_weight, new_first, new_second = adamw_update(
        master_weight, first_moment, second_moment, gradient
    )
    return (input_grads, new_weight, new_first, new_second)


def solution(mesh):
    in_specs = (
        P("pipe", None, ("dp", "fsdp"), None),
        P("pipe", None, ("dp", "fsdp"), None),
        P("pipe", ("dp", "fsdp")),
        P("pipe", "fsdp", None),
        P("pipe", "fsdp", None),
        P("pipe", "fsdp", None),
    )
    out_specs = (
        P("pipe", None, ("dp", "fsdp"), None),
        P("pipe", "fsdp", None),
        P("pipe", "fsdp", None),
        P("pipe", "fsdp", None),
    )
    return jax.shard_map(
        functools.partial(local, mesh), mesh=mesh, in_specs=in_specs, out_specs=out_specs,
        check_vma=False,
    )
```

```python
import functools

import jax
import jax.numpy as jnp
from jax import lax
from jax.experimental import pallas as pl
from jax.experimental.pallas import tpu as pltpu
from jax.sharding import PartitionSpec as P

beta_one = 0.9
beta_two = 0.95
learn_rate = 0.01
decay_rate = 0.1
adam_eps = 1e-08
loss_scale = 256.0
first_bias = 1.0 - 0.9**10
second_bias = 1.0 - 0.95**10

MESH = pl.DeviceIdType.MESH
BLOCK = 512
IN_FLIGHT = 4
COLS = 128


def adamw_update(weight_part, first_part, second_part, gradient):
    first_next = beta_one * first_part + (1.0 - beta_one) * gradient
    second_next = beta_two * second_part + (1.0 - beta_two) * gradient * gradient
    first_hat = first_next / first_bias
    second_hat = second_next / second_bias
    weight_next = weight_part - learn_rate * (
        first_hat / (jnp.sqrt(second_hat) + adam_eps) + decay_rate * weight_part
    )
    return (weight_next, first_next, second_next)


def update_kernel(
    grads_in, weight, first, second, gradient, grads_out, new_weight, new_first, new_second, sem
):
    copy = pltpu.make_async_copy(grads_in, grads_out, sem)

    @pl.when(pl.program_id(0) == 0)
    def _():
        copy.start()

    updated = adamw_update(weight[...], first[...], second[...], gradient[...])
    new_weight[...], new_first[...], new_second[...] = updated

    @pl.when(pl.program_id(0) == pl.num_programs(0) - 1)
    def _():
        copy.wait()


def kernel(
    n_pipe, n_dp, n_fsdp,
    counts_hbm, x_hbm, k_hbm, w_hbm,
    out_hbm, grad_hbm,
    counts, x, k, km, wstage, wfull, inc, res, mine, psend, precv, ysend, yrecv, xsend, xrecv,
    load_sem, chain_send, chain_recv, out_sem,
    w_send, w_recv, wf_send, wf_recv,
    p_send, p_recv, y_send, y_recv, x_send, x_recv, g_send, g_recv, grad_sem,
):
    micro, tokens, _ = x.shape
    width = k.shape[-1]
    rows = w_hbm.shape[1]
    half = rows // 2
    grad = wstage
    per_shard = micro * (rows // COLS)
    n_chunks = n_fsdp * per_shard
    per_half = half // COLS
    n_pieces = n_fsdp * per_half

    s = lax.axis_index("pipe")
    d = lax.axis_index("dp")
    f = lax.axis_index("fsdp")
    core = lax.rem(d, 2)
    core_peer = d + 1 - 2 * core
    far_peer = lax.rem(d + 2, n_dp)

    def remote(src, dst, send, recv, **where):
        return pltpu.make_async_remote_copy(
            src_ref=src, dst_ref=dst, send_sem=send, recv_sem=recv,
            device_id=where, device_id_type=MESH,
        )

    load_k = pltpu.make_async_copy(k_hbm.at[0], k, load_sem.at[0])
    load_counts = pltpu.make_async_copy(counts_hbm, counts, load_sem.at[3])
    lead, rest = pl.ds(0, COLS), pl.ds(COLS, rows - COLS)
    load_lead = pltpu.make_async_copy(w_hbm.at[0, lead], wstage.at[lead], load_sem.at[1])
    load_rest = pltpu.make_async_copy(w_hbm.at[0, rest], wstage.at[rest], load_sem.at[4])
    load_x = pltpu.make_async_copy(x_hbm.at[0], x, load_sem.at[2])
    load_counts.start()
    load_k.start()
    load_lead.start()
    load_rest.start()
    load_x.start()

    barrier = pltpu.get_barrier_semaphore()
    pl.semaphore_signal(barrier, inc=1, device_id={"dp": core_peer}, device_id_type=MESH)
    pl.semaphore_signal(barrier, inc=1, device_id={"dp": far_peer}, device_id_type=MESH)
    for i in range(1, n_fsdp):
        pl.semaphore_signal(
            barrier, inc=1, device_id={"fsdp": lax.rem(f + i, n_fsdp)}, device_id_type=MESH
        )

    @pl.when(s > 0)
    def _():
        pl.semaphore_signal(barrier, inc=1, device_id={"pipe": s - 1}, device_id_type=MESH)

    @pl.when(s < n_pipe - 1)
    def _():
        pl.semaphore_signal(barrier, inc=1, device_id={"pipe": s + 1}, device_id_type=MESH)

    load_counts.wait()
    load_k.wait()
    for m in range(micro):
        live = lax.broadcasted_iota(jnp.int32, (tokens, width), 0) < counts[0, m]
        km[m * tokens:(m + 1) * tokens, :] = jnp.where(live, k[m], jnp.zeros_like(k[m]))
    load_lead.wait()
    wfull[f, lead, :] = wstage[lead, :].astype(jnp.bfloat16)

    neighbours = n_fsdp + 1 + jnp.minimum(s, 1) + jnp.minimum(n_pipe - 1 - s, 1)
    pl.semaphore_wait(barrier, neighbours)

    my_half = pl.ds(pl.multiple_of(core * half, half), half)

    def w_copy(i):
        return remote(
            wfull.at[f, my_half], wfull.at[f, my_half], w_send.at[i - 1], w_recv.at[i - 1],
            fsdp=lax.rem(f + i, n_fsdp),
        )

    def w_forward(i):
        source = lax.rem(f + n_fsdp - i, n_fsdp)
        return remote(
            wfull.at[source, my_half], wfull.at[source, my_half],
            wf_send.at[i - 1], wf_recv.at[i - 1], dp=core_peer,
        )

    def chain_copy(j):
        return remote(res.at[j], inc.at[j], chain_send.at[j], chain_recv.at[j], pipe=s - 1)

    def place(j):
        shard = lax.rem(f + j // per_shard, n_fsdp)
        within = lax.rem(j, per_shard)
        return shard, within // micro, lax.rem(within, micro)

    def out_copy(j):
        shard, block, m = place(j)
        at = pl.ds(pl.multiple_of(shard * rows + block * COLS, COLS), COLS)
        return pltpu.make_async_copy(res.at[j], out_hbm.at[0, m, :, at], out_sem.at[j])

    def chain_step(j):
        shard, block, m = place(j)
        w_block = wfull[shard, pl.ds(pl.multiple_of(block * COLS, COLS), COLS), :]
        k_block = km[pl.ds(pl.multiple_of(m * tokens, tokens), tokens), :]
        term = lax.dot_general(
            k_block, w_block, (((1,), (1,)), ((), ())), preferred_element_type=jnp.float32
        )

        @pl.when(s < n_pipe - 1)
        def _():
            chain_copy(j).wait_recv()
            res[j] = (inc[j].astype(jnp.float32) + term).astype(jnp.bfloat16)

        @pl.when(s == n_pipe - 1)
        def _():
            res[j] = term.astype(jnp.bfloat16)

        @pl.when(s > 0)
        def _():
            chain_copy(j).start()

        out_copy(j).start()

    def chain_done(j):
        @pl.when(s > 0)
        def _():
            chain_copy(j).wait_send()

        out_copy(j).wait()

    def piece_at(q):
        return q // per_half, pl.ds(pl.multiple_of(lax.rem(q, per_half) * COLS, COLS), COLS)

    def product(q, which):
        shard = q // per_half
        start = shard * rows + which * half + lax.rem(q, per_half) * COLS
        x_block = x[:, :, pl.ds(pl.multiple_of(start, COLS), COLS)].reshape(micro * tokens, COLS)
        return lax.dot_general(
            x_block, km[...], (((0,), (0,)), ((), ())), preferred_element_type=jnp.float32
        )

    def piece_copy(q):
        shard, at = piece_at(q)
        return remote(
            psend.at[shard, at], precv.at[shard, at], p_send.at[q], p_recv.at[q], dp=core_peer
        )

    def peer_piece(q):
        shard, at = piece_at(q)
        psend[shard, at, :] = product(q, 1 - core).astype(jnp.bfloat16)
        piece_copy(q).start()

    def own_piece(q):
        shard, at = piece_at(q)
        mine[shard, at, :] = product(q, core)

    def y_copy(i):
        return remote(
            ysend.at[i - 1], yrecv.at[i - 1], y_send.at[i - 1], y_recv.at[i - 1],
            fsdp=lax.rem(f + i, n_fsdp),
        )

    x_copy = remote(xsend, xrecv, x_send, x_recv, dp=far_peer)
    g_copy = remote(grad.at[my_half], grad.at[my_half], g_send, g_recv, dp=core_peer)

    def blocks(body):
        def step(b, _):
            body(pl.ds(pl.multiple_of(b * COLS, COLS), COLS), b)
            return 0

        lax.fori_loop(0, per_half, step, 0)

    def sum_pair():
        def wait(q, _):
            piece_copy(q).wait_recv()
            return 0

        lax.fori_loop(0, n_pieces, wait, 0)
        for i in range(1, n_fsdp):
            shard = lax.rem(f + i, n_fsdp)

            def add(at, b, i=i, shard=shard):
                ysend[i - 1, at, :] = (
                    mine[shard, at, :] + precv[shard, at, :].astype(jnp.float32)
                ).astype(jnp.bfloat16)

            blocks(add)
            y_copy(i).start()

    def sum_fsdp():
        for i in range(1, n_fsdp):
            y_copy(i).wait_recv()

        def add(at, b):
            total = mine[f, at, :] + precv[f, at, :].astype(jnp.float32)
            for i in range(1, n_fsdp):
                total = total + yrecv[i - 1, at, :].astype(jnp.float32)
            xsend[at, :] = total.astype(jnp.bfloat16)

        blocks(add)
        x_copy.start()

    def sum_far():
        x_copy.wait_recv()

        def add(at, b):
            to = pl.ds(pl.multiple_of(core * half + b * COLS, COLS), COLS)
            grad[to, :] = (
                xsend[at, :].astype(jnp.float32) + xrecv[at, :].astype(jnp.float32)
            ) / loss_scale

        blocks(add)
        g_copy.start()

        def finish_pieces(q, _):
            piece_copy(q).wait_send()
            return 0

        lax.fori_loop(0, n_pieces, finish_pieces, 0)
        for i in range(1, n_fsdp):
            w_copy(i).wait_send()
            w_forward(i).wait_send()
            y_copy(i).wait_send()
        x_copy.wait_send()

    store_grad = pltpu.make_async_copy(grad, grad_hbm.at[0], grad_sem)

    def gradient_here():
        g_copy.wait_recv()
        g_copy.wait_send()
        store_grad.start()

    def forward_weights():
        for i in range(1, n_fsdp):
            w_copy(i).wait_recv()
            w_forward(i).start()

    def weights_here():
        for i in range(1, n_fsdp):
            w_forward(i).wait_recv()

    steps_a = n_pieces // 2

    def run(first, last):
        def step(j, _):
            @pl.when(j >= IN_FLIGHT)
            def _():
                chain_done(j - IN_FLIGHT)

            @pl.when(jnp.logical_or(s < n_pipe - 1, j >= micro))
            def _():
                chain_step(j)

            if last <= steps_a:
                peer_piece(2 * j)
                peer_piece(2 * j + 1)
            elif last <= 2 * steps_a:
                own_piece(2 * (j - steps_a))
                own_piece(2 * (j - steps_a) + 1)
            return 0

        if last > first:
            lax.fori_loop(first, last, step, 0)

    events = [
        (min(20, per_shard - 1), forward_weights),
        (per_shard, weights_here),
        (steps_a, None),
        (2 * steps_a, None),
        (2 * steps_a + 1, sum_pair),
        (9 * n_chunks // 16, sum_fsdp),
        (27 * n_chunks // 32, sum_far),
        (31 * n_chunks // 32, gradient_here),
    ]

    @pl.when(s == n_pipe - 1)
    def _():
        for j in range(micro):
            chain_step(j)

    load_rest.wait()

    def convert(i, _):
        at = pl.ds(pl.multiple_of(i * COLS, COLS), COLS)
        wfull[f, at, :] = wstage[at, :].astype(jnp.bfloat16)
        return 0

    lax.fori_loop(1, rows // COLS, convert, 0)
    for i in range(1, n_fsdp):
        w_copy(i).start()
    load_x.wait()
    done = 0
    for when, event in sorted(events, key=lambda pair: pair[0]):
        run(done, when)
        done = when
        if event is not None:
            event()
    run(done, n_chunks)

    for j in range(max(n_chunks - IN_FLIGHT, 0), n_chunks):
        chain_done(j)
    store_grad.wait()


def local(mesh, layer_inputs, key_grads, token_counts, master_weight, first_moment, second_moment):
    n_pipe, n_dp, n_fsdp = (mesh.shape[name] for name in ("pipe", "dp", "fsdp"))
    _, micro, tokens, features = layer_inputs.shape
    width = key_grads.shape[-1]
    rows = master_weight.shape[1]
    half = rows // 2
    n_chunks = micro * features // COLS
    n_pieces = n_fsdp * half // COLS
    others = n_fsdp - 1
    half_bf = (half, width)
    bf, f32 = jnp.bfloat16, jnp.float32
    dma = pltpu.SemaphoreType.DMA
    anywhere = pl.BlockSpec(memory_space=pl.ANY)
    input_grads, gradient = pl.pallas_call(
        functools.partial(kernel, n_pipe, n_dp, n_fsdp),
        out_shape=(
            jax.ShapeDtypeStruct(layer_inputs.shape, bf),
            jax.ShapeDtypeStruct(master_weight.shape, f32),
        ),
        in_specs=[pl.BlockSpec(memory_space=pltpu.HBM)] * 4,
        out_specs=(anywhere, anywhere),
        scratch_shapes=[
            pltpu.SMEM(token_counts.shape, jnp.int32),
            pltpu.VMEM((micro, tokens, features), bf),
            pltpu.VMEM((micro, tokens, width), bf),
            pltpu.VMEM((micro * tokens, width), bf),
            pltpu.VMEM((rows, width), f32),
            pltpu.VMEM((n_fsdp, rows, width), bf),
            pltpu.VMEM((n_chunks, tokens, COLS), bf),
            pltpu.VMEM((n_chunks, tokens, COLS), bf),
            pltpu.VMEM((n_fsdp,) + half_bf, f32),
            pltpu.VMEM((n_fsdp,) + half_bf, bf),
            pltpu.VMEM((n_fsdp,) + half_bf, bf),
            pltpu.VMEM((others,) + half_bf, bf),
            pltpu.VMEM((others,) + half_bf, bf),
            pltpu.VMEM(half_bf, bf),
            pltpu.VMEM(half_bf, bf),
            dma((5,)),
            dma((n_chunks,)), dma((n_chunks,)), dma((n_chunks,)),
            dma((others,)), dma((others,)), dma((others,)), dma((others,)),
            dma((n_pieces,)), dma((n_pieces,)),
            dma((others,)), dma((others,)),
            dma, dma, dma, dma, dma,
        ],
        compiler_params=pltpu.CompilerParams(
            collective_id=0, has_side_effects=True, vmem_limit_bytes=36 * 1024 * 1024
        ),
        cost_estimate=pl.CostEstimate(
            flops=4 * micro * tokens * width * features,
            bytes_accessed=32 * 1024 * 1024,
            transcendentals=0,
        ),
    )(
        *[
            pltpu.with_memory_space_constraint(array, pltpu.HBM)
            for array in (token_counts, layer_inputs, key_grads, master_weight)
        ]
    )
    block_rows = min(BLOCK, rows)
    block = pl.BlockSpec((1, block_rows, width), lambda i: (0, i, 0))
    state = jax.ShapeDtypeStruct(master_weight.shape, f32)
    return pl.pallas_call(
        update_kernel,
        grid=(rows // block_rows,),
        out_shape=(jax.ShapeDtypeStruct(layer_inputs.shape, bf), state, state, state),
        in_specs=[anywhere, block, block, block, block],
        out_specs=(anywhere, block, block, block),
        scratch_shapes=[dma],
        compiler_params=pltpu.CompilerParams(vmem_limit_bytes=24 * 1024 * 1024),
        cost_estimate=pl.CostEstimate(
            flops=20 * rows * width, bytes_accessed=36 * 1024 * 1024, transcendentals=rows * width
        ),
    )(input_grads, master_weight, first_moment, second_moment, gradient)


def solution(mesh):
    in_specs = (
        P("pipe", None, ("dp", "fsdp"), None),
        P("pipe", None, ("dp", "fsdp"), None),
        P("pipe", ("dp", "fsdp")),
        P("pipe", "fsdp", None),
        P("pipe", "fsdp", None),
        P("pipe", "fsdp", None),
    )
    out_specs = (
        P("pipe", None, ("dp", "fsdp"), None),
        P("pipe", "fsdp", None),
        P("pipe", "fsdp", None),
        P("pipe", "fsdp", None),
    )
    return jax.shard_map(
        functools.partial(local, mesh), mesh=mesh, in_specs=in_specs, out_specs=out_specs,
        check_vma=False,
    )
```
